32 devices in a mesh: row: 4 (over x, core), col: 8 (over z, y).
Axes of the slice: x: 2, y: 2, z: 4, core: 2. Of those that a mesh axis runs over, the one named last changes fastest.
Arguments:
- gradient: bfloat16 [4352, 8192], P('row', 'col'), may hold values from -0.03125 to 0.03125
Outputs:
- update: bfloat16 [4352, 8192], P('row', 'col')
The draws below stay inside these ranges and needn't reach their ends.
All inputs are finite; a program needn't handle non-finite values.
Results may differ from the reference program's by a relative error of at most 0.0048.
Values may be sent and summed in bfloat16 or wider, within the bound.
No kernel may reach another device: no remote copies, remote signals or barrier semaphores. Data moves between devices by JAX's collectives and lax.ppermute only.
A program may use at most 128 MiB of HBM per device.

```python
import math
import jax
import jax.numpy as jnp

M = 4352
N = 8192


def steps_of(key, dims, split, least, high):
    level = 1.0
    for axis_at, shards_of in split:
        steps = jax.random.uniform(jax.random.fold_in(jax.random.fold_in(key, 6), axis_at), (shards_of,), jnp.float32, least / len(split), high / len(split))
        level = level * jnp.repeat(jnp.exp(steps), dims[axis_at] // shards_of).reshape((-1,) + (1,) * (len(dims) - 1 - axis_at))
    return level


def bell_draw(stream_key, dims, scale, bound, cuts=(), kind=jnp.bfloat16):
    gain = steps_of(stream_key, dims, cuts, -0.22, 0.18) if cuts else 1.0
    result = jax.random.normal(stream_key, dims, jnp.float32) * scale * gain
    return jnp.minimum(jnp.maximum(result, -bound), bound).astype(kind)


def setup_inputs(seed: int = 0) -> dict:
    arg_keys = jax.random.split(jax.random.key(seed), 2)
    gradient = bell_draw(arg_keys[0], (M, N), (4 * N) ** -0.5, 0.03125, ((0, 4), (1, 8)))
    return dict(gradient=gradient)


A_COEF = 3.4445
B_COEF = -4.775
C_COEF = 2.0315

def reference(gradient):
    gram_matrix = jnp.dot(gradient, gradient.T, preferred_element_type=jnp.float32).astype(jnp.bfloat16)
    square = jnp.dot(gram_matrix, gram_matrix, preferred_element_type=jnp.float32)
    poly_matrix = (B_COEF * gram_matrix.astype(jnp.float32) + C_COEF * square).astype(jnp.bfloat16)
    product = jnp.dot(poly_matrix, gradient, preferred_element_type=jnp.float32)
    rms_scale = math.sqrt(N)
    return (rms_scale * (A_COEF * gradient.astype(jnp.float32) + product)).astype(jnp.bfloat16)
```

```python
import math

import jax
import jax.numpy as jnp
from jax import lax
from jax.sharding import PartitionSpec as P

A_COEF = 3.4445
B_COEF = -4.775
C_COEF = 2.0315

ROWS_BY_ROWS = (((1,), (1,)), ((), ()))
PLAIN = (((1,), (0,)), ((), ()))
LEFT_TURNED = (((0,), (0,)), ((), ()))


def product(left, right, dims):
    return lax.dot_general(left, right, dims, preferred_element_type=jnp.float32)


def from_row(value, source):
    count = lax.axis_size("row")
    return lax.ppermute(value, "row", [(source(i), i) for i in range(count)])


def from_col(value, mask):
    count = lax.axis_size("col")
    return lax.ppermute(value, "col", [(i ^ mask, i) for i in range(count)])


def partner(mate):
    top = 1 << (mate.bit_length() - 1)
    return lambda i: i ^ mate ^ (1 if i & top else 0)


def shards(gradient):
    rows = gradient.shape[0]
    row_count = lax.axis_size("row")
    col_count = lax.axis_size("col")
    z_count = col_count // 2
    half = rows // 2
    quarter = half // z_count
    col = lax.axis_index("col")
    y, z = col % 2, col // 2
    mates = range(2, row_count, 2)

    crossed = [from_row(gradient, partner(m)) for m in mates]
    mine = lax.dynamic_slice_in_dim(gradient, y * half, half, 0)
    other = lax.dynamic_slice_in_dim(gradient, (1 - y) * half, half, 0)

    def scatter(right):
        sent = product(other, right, ROWS_BY_ROWS).astype(jnp.bfloat16)
        got = from_col(sent, 1)
        pair = (product(mine, right, ROWS_BY_ROWS) + got.astype(jnp.float32)).astype(jnp.bfloat16)
        total = lax.dynamic_slice_in_dim(pair, z * quarter, quarter, 0).astype(jnp.float32)
        for m in range(1, z_count):
            piece = lax.dynamic_slice_in_dim(pair, (z ^ m) * quarter, quarter, 0)
            total = total + from_col(piece, 2 * m).astype(jnp.float32)
        return total.astype(jnp.bfloat16)

    def gather(shard):
        held = jnp.zeros((half, shard.shape[1]), shard.dtype)
        held = lax.dynamic_update_slice_in_dim(held, shard, z * quarter, 0)
        for m in range(1, z_count):
            held = lax.dynamic_update_slice_in_dim(held, from_col(shard, 2 * m), (z ^ m) * quarter, 0)
        return held, from_col(held, 1)

    def whole(mine_half, other_half):
        first = jnp.where(y == 0, mine_half, other_half)
        second = jnp.where(y == 0, other_half, mine_half)
        return jnp.concatenate([first, second], 0)

    swap = lambda value: from_row(value, lambda i: i ^ 1)
    beside = swap(gradient)
    near = [gradient, beside]
    near_shards = [scatter(right) for right in near]
    near_blocks = [gather(shard) for shard in near_shards]
    far_shards = [scatter(right) for right in crossed]
    turned_shards = [from_row(shard, lambda i, m=m: _inverse(partner(m), row_count)[i]) for m, shard in zip(mates, far_shards)]
    turned = [whole(*gather(shard)) for shard in turned_shards]
    far_blocks = [gather(shard) for shard in far_shards]
    crossed_beside = [swap(value) for value in crossed]

    def rows_times(at, values, turned_sum):
        own, next_to, over, over_beside = values
        total = turned_sum
        for block, right in zip(near_blocks + far_blocks, [own, next_to] + over):
            total = total + product(block[at], right, PLAIN)
        return total

    turned_sum = sum(product(block, right, LEFT_TURNED) for block, right in zip(turned, crossed_beside))
    values = (gradient, beside, crossed, crossed_beside)

    def of_half(value, at):
        return lax.dynamic_slice_in_dim(value, (y if at == 0 else 1 - y) * half, half, 0)

    inner = []
    for at in (0, 1):
        start = of_half(gradient, at).astype(jnp.float32)
        inner.append((B_COEF * start + C_COEF * rows_times(at, values, of_half(turned_sum, at))).astype(jnp.bfloat16))
    inner_crossed = [whole(*[from_row(part, partner(m)) for part in inner]) for m in mates]
    inner_own = whole(*inner)
    inner_values = (inner_own, swap(inner_own), inner_crossed, [swap(value) for value in inner_crossed])
    turned_sum = sum(product(block, right, LEFT_TURNED) for block, right in zip(turned, inner_values[3]))
    rms_scale = math.sqrt(gradient.shape[1] * col_count)
    out = []
    for at in (0, 1):
        start = of_half(gradient, at).astype(jnp.float32)
        out.append((rms_scale * (A_COEF * start + rows_times(at, inner_values, of_half(turned_sum, at)))).astype(jnp.bfloat16))
    return whole(*out)


def _inverse(source, count):
    table = {source(i): i for i in range(count)}
    return [table[i] for i in range(count)]


def solution(mesh):
    spec = P("row", "col")
    return jax.shard_map(shards, mesh=mesh, in_specs=(spec,), out_specs=spec, check_vma=False)
```

```python
import math

import jax
import jax.numpy as jnp
from jax import lax
from jax.sharding import PartitionSpec as P

A_COEF = 3.4445
B_COEF = -4.775
C_COEF = 2.0315

ROWS_BY_ROWS = (((1,), (1,)), ((), ()))
PLAIN = (((1,), (0,)), ((), ()))
LEFT_TURNED = (((0,), (0,)), ((), ()))


def product(left, right, dims):
    return lax.dot_general(left, right, dims, preferred_element_type=jnp.float32)


def from_row(value, source):
    count = lax.axis_size("row")
    return lax.ppermute(value, "row", [(source(i), i) for i in range(count)])


def from_col(value, mask):
    count = lax.axis_size("col")
    return lax.ppermute(value, "col", [(i ^ mask, i) for i in range(count)])


def swap(value):
    return from_row(value, lambda i: i ^ 1)


def partner(mate):
    top = 1 << (mate.bit_length() - 1)
    return lambda i: i ^ mate ^ (1 if i & top else 0)


def inverse(source, count):
    table = {source(i): i for i in range(count)}
    return table.__getitem__


class Sequence:
    def __init__(self):
        self.last = None

    def __call__(self, name, step, *values):
        if self.last is not None:
            values = lax.optimization_barrier((values, self.last))[0]
        with jax.named_scope(name):
            result = step(*values)
        self.last = jax.tree.leaves(result)[0]
        return result


def take(value, at, count):
    return lax.dynamic_slice_in_dim(value, at * count, count, 0)


def joined(mine, other, at):
    count = mine.shape[0]
    both = lax.dynamic_update_slice_in_dim(jnp.zeros((2 * count, mine.shape[1]), mine.dtype), mine, at * count, 0)
    return lax.dynamic_update_slice_in_dim(both, other, (1 - at) * count, 0)


def shards(gradient):
    kept_rows = gradient.shape[0]
    row_count = lax.axis_size("row")
    col_count = lax.axis_size("col")
    gradient = jnp.pad(gradient, ((0, -kept_rows % col_count), (0, 0)))
    rows = gradient.shape[0]
    col = lax.axis_index("col")
    masks = [1 << b for b in range(col_count.bit_length() - 1)]
    y_first = masks
    z_first = masks[1:] + masks[:1]
    mates = range(2, row_count, 2)
    run = Sequence()

    def bit(mask):
        return col // mask % 2

    class Piece:
        def __init__(self, name, order):
            self.name, self.order = name, order

        def start(self, right):
            mask = self.order[0]
            half = rows // 2
            self.right = right
            self.sent = run(self.name + "_sent", lambda left, right: product(take(left, 1 - bit(mask), half), right, ROWS_BY_ROWS).astype(jnp.bfloat16), gradient, right)
            self.got = from_col(self.sent, mask)

        def keep(self):
            mask = self.order[0]
            half = rows // 2
            self.kept = run(self.name + "_kept", lambda left, right: product(take(left, bit(mask), half), right, ROWS_BY_ROWS), gradient, self.right)
            self.step = 1

        def halve(self):
            mask = self.order[self.step]
            count = self.kept.shape[0] // 2

            def one(kept, got):
                total = kept + got.astype(jnp.float32)
                return take(total, 1 - bit(mask), count).astype(jnp.bfloat16), take(total, bit(mask), count)

            sent, self.kept = run(f"{self.name}_halved_{self.step}", one, self.kept, self.got)
            self.got = from_col(sent, mask)
            self.step += 1

        def finish(self):
            self.shard = run(self.name + "_shard", lambda kept, got: (kept + got.astype(jnp.float32)).astype(jnp.bfloat16), self.kept, self.got)
            self.spread(self.shard)

        def spread(self, shard):
            self.held = shard
            self.step = len(self.order) - 1
            self.got = from_col(shard, self.order[self.step])

        def double(self):
            mask = self.order[self.step]
            self.held = run(f"{self.name}_doubled_{self.step}", lambda held, got: joined(held, got, bit(mask)), self.held, self.got)
            self.step -= 1
            if self.step >= 0:
                self.got = from_col(self.held, self.order[self.step])

    own, near = Piece("own", z_first), Piece("next", y_first)
    far = [Piece(f"far_{m}", y_first) for m in mates]
    turned = [Piece(f"turned_{m}", y_first) for m in mates]
    steps = len(masks)

    crossed = [from_row(gradient, partner(m)) for m in mates]
    beside = swap(gradient)
    own.start(gradient)
    near.start(beside)
    own.keep()
    near.keep()
    own.halve()
    near.halve()
    for piece, right in zip(far, crossed):
        piece.start(right)
        piece.keep()
    crossed_beside = [swap(value) for value in crossed]
    for _ in range(steps - 2):
        own.halve()
        near.halve()
    own.finish()
    near.finish()
    for piece in far:
        piece.halve()
    own.double()
    near.double()
    for _ in range(steps - 2):
        for piece in far:
            piece.halve()
        own.double()
        near.double()
    for piece, other, m in zip(far, turned, mates):
        piece.finish()
        other.spread(from_row(piece.shard, inverse(partner(m), row_count)))
    own.double()
    near.double()
    inner = run("inner_own", lambda block, right: product(block, right, PLAIN), own.held, gradient)
    inner = run("inner_next", lambda total, block, right: total + product(block, right, PLAIN), inner, near.held, beside)
    for _ in range(steps - 1):
        for piece in turned:
            piece.double()
        for piece in far:
            piece.double()
    half = rows // 2
    at = bit(masks[0])
    for piece, right in zip(turned, crossed_beside):
        piece.double()
        inner = run("inner_turned", lambda total, block, right: total + product(block, right, LEFT_TURNED), inner, piece.held, right)

    def finish_inner(total, start, side, *blocks):
        total = take(total, side, half)
        for block, right in zip(blocks, crossed):
            total = total + product(block, right, PLAIN)
        return (B_COEF * take(start, side, half).astype(jnp.float32) + C_COEF * total).astype(jnp.bfloat16)

    inner_mine = run("inner_mine", lambda total, start, *blocks: finish_inner(total, start, at, *blocks), inner, gradient, *[piece.held for piece in far])
    mine_crossed = [from_row(inner_mine, partner(m)) for m in mates]
    inner_other = run("inner_other", lambda total, start, *blocks: finish_inner(total, start, 1 - at, *blocks), inner, gradient, *[piece.got for piece in far])
    other_crossed = [from_row(inner_other, partner(m)) for m in mates]
    inner = run("inner_whole", lambda a, b: joined(a, b, at), inner_mine, inner_other)
    inner_beside = swap(inner)
    for piece in far:
        piece.double()
    outer = run("outer_own", lambda block, right: product(block, right, PLAIN), own.held, inner)
    outer = run("outer_next", lambda total, block, right: total + product(block, right, PLAIN), outer, near.held, inner_beside)
    whole_crossed = [run("crossed_whole", lambda a, b: joined(a, b, at), a, b) for a, b in zip(mine_crossed, other_crossed)]
    whole_beside = [swap(value) for value in whole_crossed]
    for piece, right in zip(far, whole_crossed):
        outer = run("outer_far", lambda total, block, right: total + product(block, right, PLAIN), outer, piece.held, right)
    rms_scale = math.sqrt(gradient.shape[1] * col_count)

    def finish_outer(total, start, *pairs):
        count = len(pairs) // 2
        for block, right in zip(pairs[:count], pairs[count:]):
            total = total + product(block, right, LEFT_TURNED)
        return (rms_scale * (A_COEF * start.astype(jnp.float32) + total)).astype(jnp.bfloat16)

    return run("update", finish_outer, outer, gradient, *[piece.held for piece in turned], *whole_beside)[:kept_rows]


def solution(mesh):
    spec = P("row", "col")
    return jax.shard_map(shards, mesh=mesh, in_specs=(spec,), out_specs=spec, check_vma=False)
```

```python
import heapq
import math

import jax
import jax.numpy as jnp
from jax import lax
from jax.sharding import PartitionSpec as P

A_COEF = 3.4445
B_COEF = -4.775
C_COEF = 2.0315

ROWS_BY_ROWS = (((1,), (1,)), ((), ()))
PLAIN = (((1,), (0,)), ((), ()))
LEFT_TURNED = (((0,), (0,)), ((), ()))

STEP_COST = 7.0
NEAR_COST = 60.0
FAR_COST = 50.0
BESIDE_COST = 9.0
CROSSED_COST = 50.0
CROSSED_BESIDE_AT = 90.0


def product(left, right, dims):
    return lax.dot_general(left, right, dims, preferred_element_type=jnp.float32)


def from_row(value, source):
    count = lax.axis_size("row")
    return lax.ppermute(value, "row", [(source(i), i) for i in range(count)])


def from_col(value, mask):
    count = lax.axis_size("col")
    return lax.ppermute(value, "col", [(i ^ mask, i) for i in range(count)])


def swap(value):
    return from_row(value, lambda i: i ^ 1)


def partner(mate):
    top = 1 << (mate.bit_length() - 1)
    return lambda i: i ^ mate ^ (1 if i & top else 0)


def inverse(source, count):
    table = {source(i): i for i in range(count)}
    return table.__getitem__


class Sequence:
    def __init__(self):
        self.last = None
        self.agenda = []
        self.added = 0

    def __call__(self, name, step, *values):
        if self.last is not None:
            values = lax.optimization_barrier((values, self.last))[0]
        with jax.named_scope(name):
            result = step(*values)
        self.last = jax.tree.leaves(result)[0]
        return result

    def hold(self, value):
        value, _ = lax.optimization_barrier((value, self.last))
        self.last = value
        return value

    def at(self, time, step):
        heapq.heappush(self.agenda, (time, self.added, step))
        self.added += 1

    def drain(self):
        while self.agenda:
            time, _, step = heapq.heappop(self.agenda)
            step(time)


def take(value, at, count):
    return lax.dynamic_slice_in_dim(value, at * count, count, 0)


def joined(mine, other, at, axis=0):
    count = mine.shape[axis]
    shape = mine.shape[:axis] + (2 * count,) + mine.shape[axis + 1 :]
    both = lax.dynamic_update_slice_in_dim(jnp.zeros(shape, mine.dtype), mine, at * count, axis)
    if other is None:
        return both
    return lax.dynamic_update_slice_in_dim(both, other, (1 - at) * count, axis)


class Scatter:
    def __init__(self, run, name, masks, cost, left, right, bit, done):
        self.cost, self.run, self.name, self.masks, self.left, self.right, self.bit, self.done = cost, run, name, masks, left, right, bit, done
        self.share = right.shape[0] / left.shape[0]

    def start(self, time):
        mask, half = self.masks[0], self.left.shape[0] // 2
        at = self.bit(mask)

        def sent(left, right):
            return product(take(left, 1 - at, half), right, ROWS_BY_ROWS).astype(jnp.bfloat16)

        def kept(left, right):
            return product(take(left, at, half), right, ROWS_BY_ROWS)

        self.got = from_col(self.run(self.name + "_sent", sent, self.left, self.right), mask)
        self.kept = self.run(self.name + "_kept", kept, self.left, self.right)
        self.step = 1
        self.run.at(time + STEP_COST + self.cost * self.share / 2, self.halve)

    def halve(self, time):
        if self.step == len(self.masks):
            shard = self.run(self.name + "_shard", lambda kept, got: (kept + got.astype(jnp.float32)).astype(jnp.bfloat16), self.kept, self.got)
            return self.done(time, shard)
        mask, count = self.masks[self.step], self.kept.shape[0] // 2
        at = self.bit(mask)

        def one(kept, got):
            total = kept + got.astype(jnp.float32)
            return take(total, 1 - at, count).astype(jnp.bfloat16), take(total, at, count)

        sent, self.kept = self.run(f"{self.name}_halved_{self.step}", one, self.kept, self.got)
        self.got = from_col(sent, mask)
        self.step += 1
        self.run.at(time + STEP_COST + self.cost * self.share / 2**self.step, self.halve)


class Gather:
    def __init__(self, run, name, masks, steps, cost, bit, shard, done=None, stop=0):
        self.run, self.name, self.masks, self.steps, self.bit, self.done, self.stop = run, name, masks, list(steps), bit, done, stop
        self.held = shard.reshape((1,) * len(masks) + shard.shape)
        self.share = cost * shard.shape[1] / shard.shape[0] / 4 ** len(masks)

    def start(self, time):
        if self.done is not None and len(self.steps) == self.stop:
            self.done(time)
        if self.steps:
            self.got = from_col(self.held, self.steps[0])
            if len(self.steps) > self.stop:
                self.run.at(time + STEP_COST + self.share, self.double)

    def double(self, time):
        mask = self.steps.pop(0)
        axis, at = self.masks.index(mask), self.bit(mask)
        self.held = self.run(f"{self.name}_doubled_{len(self.steps)}", lambda held, got: joined(held, got, at, axis), self.held, self.got)
        self.share *= 2
        self.start(time)

    @property
    def block(self):
        return self.held.reshape(-1, self.held.shape[-1])


def shards(gradient):
    kept_rows = gradient.shape[0]
    row_count = lax.axis_size("row")
    col_count = lax.axis_size("col")
    gradient = jnp.pad(gradient, ((0, -kept_rows % col_count), (0, 0)))
    rows = gradient.shape[0]
    half = rows // 2
    col = lax.axis_index("col")
    masks = [1 << b for b in range(col_count.bit_length() - 1)]
    y_first, z_first = masks, masks[1:] + masks[:1]
    y_last = masks[::-1]
    z_last = masks[:1] + masks[:0:-1]
    mates = range(2, row_count, 2)
    run = Sequence()

    def bit(mask):
        return col // mask % 2

    at = bit(masks[0])
    cut = half // 128 * 128
    bounds = [(0, cut), (cut, rows)] if cut else [(0, rows)]
    beside = swap(gradient)
    sent_parts = []

    def send_part(time):
        a, b = bounds[len(sent_parts)]
        sent_parts.append(run("part", lambda value: value[a:b], gradient))

    send_part(0)
    own = Scatter(run, "own", z_first, NEAR_COST, gradient, gradient, bit, lambda time, shard: gather("own", z_first, y_last, NEAR_COST, done=add_inner("own", "own", gradient))(time, shard))
    own.start(0)
    for _ in bounds[1:]:
        send_part(0)
    crossed_parts = [[from_row(part, partner(m)) for part in sent_parts] for m in mates]
    crossed_beside_parts = [[None] * len(bounds) for m in mates]
    gathers = {}
    turned = {}
    inner = []

    def add_inner(name, left, right):
        def add(time):
            block = gathers[name].block
            if inner:
                inner[0] = run("inner_" + name, lambda total, block, right: total + product(block, right, PLAIN), inner[0], block, right)
            else:
                inner.append(run("inner_" + name, lambda block, right: product(block, right, PLAIN), block, right))

        return add

    def gather(name, masks, steps, cost, stop=0, done=None):
        def begin(time, shard):
            gathers[name] = Gather(run, name, masks, steps, cost, bit, shard, stop=stop, done=done)
            gathers[name].start(time)

        return begin

    def part_done(m, index):
        name = f"far_{m}_{index}"
        source = inverse(partner(m), row_count)

        def over(value, time, place):
            moved = from_row(value, source)
            run.at(time + STEP_COST + CROSSED_COST / 4, lambda time: turned.__setitem__((m, index, place), run.hold(moved)))

        def arrived(time):
            piece = gathers[name]
            piece.got = run.hold(piece.got)
            over(piece.got, time, 1)

        def mine_done(time):
            over(gathers[name].held, time, 0)
            run.at(time + STEP_COST + FAR_COST / 4, arrived)

        return lambda time, shard: gather(name, y_first, y_last, FAR_COST, stop=1, done=mine_done)(time, shard)

    def far_start(m, index, part):
        scatter = Scatter(run, f"far_{m}_{index}", y_first, FAR_COST, gradient, part, bit, part_done(m, index))

        def start(time):
            scatter.start(time)

        return start

    def start_beside(time):
        for values, kept in zip(crossed_parts, crossed_beside_parts):
            for index, value in enumerate(values):
                run.at(time + 2 * BESIDE_COST, lambda time, kept=kept, index=index, value=swap(run.hold(value)): kept.__setitem__(index, run.hold(value)))

    run.at(CROSSED_BESIDE_AT, start_beside)
    run.at(BESIDE_COST, Scatter(run, "next", y_first, NEAR_COST, gradient, beside, bit, gather("next", y_first, z_last, NEAR_COST, done=add_inner("next", "next", beside))).start)
    for m, parts in zip(mates, crossed_parts):
        for index, (part, (_, end)) in enumerate(zip(parts, bounds)):
            run.at(STEP_COST + CROSSED_COST * end / rows, far_start(m, index, part))
    run.drain()

    inner = inner[0]
    own, near = gathers["own"].block, gathers["next"].block
    parts = range(len(bounds))
    beside_columns = lambda *values: jnp.concatenate(values, -1)
    whole_columns = lambda *values: joined(*[jnp.concatenate(values[i :: 2], -1).reshape(half, rows) for i in (0, 1)], at)
    turned = [run("turned_whole", whole_columns, *[turned[m, i, place] for i in parts for place in (0, 1)]) for m in mates]
    below = lambda *values: jnp.concatenate(values, 0)
    crossed_beside = [run("crossed_beside_whole", below, *values) for values in crossed_beside_parts]
    for block, right in zip(turned, crossed_beside):
        inner = run("inner_turned", lambda total, block, right: total + product(block, right, LEFT_TURNED), inner, block, right)
    crossed = [run("crossed_whole", below, *values) for values in crossed_parts]
    far_mine = [run("far_mine", beside_columns, *[gathers[f"far_{m}_{i}"].held.reshape(half, -1) for i in parts]) for m in mates]

    def finish_inner(total, start, side, *blocks):
        total = take(total, side, half)
        for block, right in zip(blocks, crossed):
            total = total + product(block, right, PLAIN)
        return (B_COEF * take(start, side, half).astype(jnp.float32) + C_COEF * total).astype(jnp.bfloat16)

    mine = run("inner_mine", lambda total, start, *blocks: finish_inner(total, start, at, *blocks), inner, gradient, *far_mine)
    mine_crossed = [from_row(mine, partner(m)) for m in mates]
    far_other = [run("far_other", beside_columns, *[gathers[f"far_{m}_{i}"].got.reshape(half, -1) for i in parts]) for m in mates]
    other = run("inner_other", lambda total, start, *blocks: finish_inner(total, start, 1 - at, *blocks), inner, gradient, *far_other)
    other_crossed = [from_row(other, partner(m)) for m in mates]
    inner = run("inner_whole", lambda a, b: joined(a, b, at), mine, other)
    inner_beside = swap(inner)
    far = [run("far_whole", lambda a, b: joined(a, b, at), a, b) for a, b in zip(far_mine, far_other)]
    mine_crossed = [run.hold(value) for value in mine_crossed]
    mine_beside = [swap(value) for value in mine_crossed]
    outer = run("outer_own", lambda block, right: product(block, right, PLAIN), own, inner)
    outer = run("outer_next", lambda total, block, right: total + product(block, right, PLAIN), outer, near, inner_beside)

    def add_far(total, block, right, side):
        return total + product(block, joined(right, None, side), PLAIN)

    for block, right in zip(far, mine_crossed):
        outer = run("outer_far_mine", lambda total, block, right: add_far(total, block, right, at), outer, block, right)
    for block, right in zip(turned, mine_beside):
        outer = run("outer_turned_mine", lambda total, block, right: total + product(take(block, at, half), right, LEFT_TURNED), outer, block, right)
    other_crossed = [run.hold(value) for value in other_crossed]
    other_beside = [swap(value) for value in other_crossed]
    for block, right in zip(far, other_crossed):
        outer = run("outer_far_other", lambda total, block, right: add_far(total, block, right, 1 - at), outer, block, right)
    rms_scale = math.sqrt(gradient.shape[1] * col_count)

    def finish_outer(total, start, *pairs):
        count = len(pairs) // 2
        for block, right in zip(pairs[:count], pairs[count:]):
            total = total + product(take(block, 1 - at, half), right, LEFT_TURNED)
        return (rms_scale * (A_COEF * start.astype(jnp.float32) + total)).astype(jnp.bfloat16)

    return run("update", finish_outer, outer, gradient, *turned, *other_beside)[:kept_rows]


def solution(mesh):
    spec = P("row", "col")
    return jax.shard_map(shards, mesh=mesh, in_specs=(spec,), out_specs=spec, check_vma=False)
```

```python
import heapq
import math

import jax
import jax.numpy as jnp
from jax import lax
from jax.sharding import PartitionSpec as P

A_COEF = 3.4445
B_COEF = -4.775
C_COEF = 2.0315

ROWS_BY_ROWS = (((1,), (1,)), ((), ()))
PLAIN = (((1,), (0,)), ((), ()))
LEFT_TURNED = (((0,), (0,)), ((), ()))

STARTS = {"own": 0.0, "next": 17.0, "far_0": 30.0, "far_1": 58.0}
SCATTERS = {"own": (40.0, 25.0, 18.0), "next": (24.0, 24.0, 17.0), "far_0": (22.0, 18.0, 15.0), "far_1": (20.0, 13.0, 9.0)}
GATHERS = {"own": (14.0, 18.0, 32.0), "next": (8.0, 20.0, 25.0), "far_0": (11.0, 11.0, 18.0), "far_1": (8.0, 14.0, 20.0)}
DELAYS = {"own": 104.0, "next": 106.0}
OVER_COST = 18.0
CROSSED_BESIDE_AT = 60.0
CROSSED_BESIDE_COST = 18.0
MIRROR_COST = 12.0


def cost(table, kind, step):
    return table[kind][min(step, len(table[kind]) - 1)]


def product(left, right, dims):
    return lax.dot_general(left, right, dims, preferred_element_type=jnp.float32)


def from_row(value, source):
    count = lax.axis_size("row")
    return lax.ppermute(value, "row", [(source(i), i) for i in range(count)])


def from_col(value, mask):
    count = lax.axis_size("col")
    return lax.ppermute(value, "col", [(i ^ mask, i) for i in range(count)])


def swap(value):
    return from_row(value, lambda i: i ^ 1)


def partner(mate):
    top = 1 << (mate.bit_length() - 1)
    return lambda i: i ^ mate ^ (1 if i & top else 0)


def inverse(source, count):
    table = {source(i): i for i in range(count)}
    return table.__getitem__


class Sequence:
    def __init__(self):
        self.last = None
        self.agenda = []
        self.added = 0

    def __call__(self, name, step, *values):
        if self.last is not None:
            values = lax.optimization_barrier((values, self.last))[0]
        with jax.named_scope(name):
            result = step(*values)
        self.last = jax.tree.leaves(result)[0]
        return result

    def hold(self, value):
        value, _ = lax.optimization_barrier((value, self.last))
        self.last = value
        return value

    def tie(self, value):
        return lax.optimization_barrier((value, self.last))[0]

    def at(self, time, step):
        heapq.heappush(self.agenda, (time, self.added, step))
        self.added += 1

    def drain(self):
        while self.agenda:
            time, _, step = heapq.heappop(self.agenda)
            step(time)


def take(value, at, count):
    return lax.dynamic_slice_in_dim(value, at * count, count, 0)


def joined(mine, other, at, axis=0):
    count = mine.shape[axis]
    shape = mine.shape[:axis] + (2 * count,) + mine.shape[axis + 1 :]
    both = lax.dynamic_update_slice_in_dim(jnp.zeros(shape, mine.dtype), mine, at * count, axis)
    if other is None:
        return both
    return lax.dynamic_update_slice_in_dim(both, other, (1 - at) * count, axis)


class Scatter:
    def __init__(self, run, name, kind, masks, left, right, bit, done, twist=None):
        self.run, self.name, self.kind, self.masks, self.left, self.right, self.bit, self.done = run, name, kind, masks, left, right, bit, done
        self.twist = twist

    def start(self, time):
        mask, half = self.masks[0], self.left.shape[0] // 2
        at = self.bit(mask)

        def columns(right, place):
            return right if self.twist is None else take(right, place ^ self.twist, half)

        def sent(left, right):
            return product(take(left, 1 - at, half), columns(right, 1 - at), ROWS_BY_ROWS).astype(jnp.bfloat16)

        def kept(left, right):
            return product(take(left, at, half), columns(right, at), ROWS_BY_ROWS)

        self.got = from_col(self.run(self.name + "_sent", sent, self.left, self.right), mask)
        self.kept = self.run(self.name + "_kept", kept, self.left, self.right)
        self.step = 1
        self.run.at(time + cost(SCATTERS, self.kind, 0), self.halve)

    def halve(self, time):
        if self.step == len(self.masks):
            shard = self.run(self.name + "_shard", lambda kept, got: (kept + got.astype(jnp.float32)).astype(jnp.bfloat16), self.kept, self.got)
            return self.done(time, shard)
        mask, count = self.masks[self.step], self.kept.shape[0] // 2
        at = self.bit(mask)

        def one(kept, got):
            total = kept + got.astype(jnp.float32)
            return take(total, 1 - at, count).astype(jnp.bfloat16), take(total, at, count)

        sent, self.kept = self.run(f"{self.name}_halved_{self.step}", one, self.kept, self.got)
        self.got = from_col(sent, mask)
        self.step += 1
        self.run.at(time + cost(SCATTERS, self.kind, self.step - 1), self.halve)


def checkered(block, mirror, right, core):
    half = block.shape[0] // 2
    rows = [product(block[:half], take(right, core, half), PLAIN), product(block[half:], take(right, 1 - core, half), PLAIN)]
    turned = [product(mirror[:half], right[:half], LEFT_TURNED), product(mirror[half:], right[half:], LEFT_TURNED)]
    swapped = core == 0
    return jnp.concatenate([rows[0] + jnp.where(swapped, turned[1], turned[0]), rows[1] + jnp.where(swapped, turned[0], turned[1])], 0)


class Gather:
    def __init__(self, run, name, kind, masks, steps, bit, shard, done=None, stop=0):
        self.run, self.name, self.kind, self.masks, self.steps, self.bit, self.done, self.stop = run, name, kind, masks, list(steps), bit, done, stop
        self.held = shard.reshape((1,) * len(masks) + shard.shape)
        self.taken = 0

    def start(self, time):
        if self.done is not None and len(self.steps) == self.stop:
            self.done(time)
        if self.steps:
            self.got = from_col(self.held, self.steps[0])
            if len(self.steps) > self.stop:
                self.run.at(time + cost(GATHERS, self.kind, self.taken), self.double)

    def double(self, time):
        mask = self.steps.pop(0)
        axis, at = self.masks.index(mask), self.bit(mask)
        self.held = self.run(f"{self.name}_doubled_{len(self.steps)}", lambda held, got: joined(held, got, at, axis), self.held, self.got)
        self.taken += 1
        self.start(time)

    @property
    def block(self):
        return self.held.reshape(-1, self.held.shape[-1])


def shards(gradient):
    kept_rows = gradient.shape[0]
    row_count = lax.axis_size("row")
    col_count = lax.axis_size("col")
    gradient = jnp.pad(gradient, ((0, -kept_rows % col_count), (0, 0)))
    rows = gradient.shape[0]
    half = rows // 2
    col = lax.axis_index("col")
    masks = [1 << b for b in range(col_count.bit_length() - 1)]
    y_first, z_first = masks, masks[1:] + masks[:1]
    y_last = masks[::-1]
    z_last = masks[:1] + masks[:0:-1]
    mates = range(2, row_count, 2)
    run = Sequence()

    def bit(mask):
        return col // mask % 2

    at = bit(masks[0])
    cut = half // 128 * 128
    bounds = [(0, cut), (cut, rows)] if cut else [(0, rows)]
    beside = swap(gradient)
    gathers = {}
    turned = {}
    near, totals, turned_parts, inner_parts, inner_crossed = [], [], {}, {}, {}
    crossed, crossed_beside = {}, {}
    core = lax.axis_index("row") % 2
    missing = [2 + len(mates) * len(bounds)]

    def add_total(name, step, *values):
        if totals:
            totals[0] = run(name, lambda total, *values: total + step(*values), totals[0], *values)
        else:
            totals.append(run(name, step, *values))
        missing[0] -= 1
        finish_parts()

    def finish_parts():
        for index, (a, b) in enumerate(bounds):
            if missing[0] or index in inner_parts or len(turned_parts.get(index, ())) < len(mates):
                continue

            def finish(total, start, *values):
                total = total[a:b]
                for block, right in zip(values[: len(mates)], values[len(mates) :]):
                    total = total + product(block, right, LEFT_TURNED)
                return (B_COEF * start[a:b].astype(jnp.float32) + C_COEF * total).astype(jnp.bfloat16)

            part = run("inner_part", finish, totals[0], gradient, *[turned_parts[index][m] for m in mates], *[crossed_beside[m] for m in mates])
            inner_parts[index] = part
            inner_crossed[index] = [from_row(part, partner(m)) for m in mates]

    def add_own(time):
        add_total("inner_own", lambda block, right: product(block, right, PLAIN), gathers["own"].block, gradient)

    def add_next(time):
        near.append(gathers["next"].block)
        mirror = swap(near[0])

        def add(time):
            near.append(mirror)
            add_total("inner_next", lambda *values: checkered(*values, core), *near, beside)

        run.at(time + MIRROR_COST, add)

    def as_block(mine, other):
        return joined(mine.reshape(half, -1), other.reshape(half, -1), at)

    def gather(name, kind, masks, steps, stop=0, done=None):
        def begin(time, shard):
            piece = gathers[name] = Gather(run, name, kind, masks, steps, bit, shard, stop=stop, done=done)

            def start(time):
                piece.held = run.tie(piece.held)
                piece.start(time)

            if kind in DELAYS:
                run.at(max(time, DELAYS[kind]), start)
            else:
                piece.start(time)

        return begin

    far_blocks = {}

    def part_done(m, index):
        name = f"far_{m}_{index}"
        source = inverse(partner(m), row_count)

        def over(value, time, place):
            moved = from_row(value, source)

            def take_in(time):
                turned[m, index, place] = run.hold(moved)
                if (m, index, 0) in turned and (m, index, 1) in turned:
                    turned_parts.setdefault(index, {})[m] = run("turned_part", as_block, turned[m, index, 0], turned[m, index, 1])
                    finish_parts()

            run.at(time + OVER_COST, take_in)

        def arrived(time):
            piece = gathers[name]
            got = run.hold(piece.got)
            over(got, time, 1)
            far_blocks[m, index] = run("far_block", as_block, piece.held, got)
            a, b = bounds[index]
            add_total("inner_far", lambda block, right: product(block, right[a:b], PLAIN), far_blocks[m, index], crossed[m])

        def mine_done(time):
            over(gathers[name].held, time, 0)
            run.at(time + cost(GATHERS, f"far_{index}", 2), arrived)

        return gather(name, f"far_{index}", y_first, y_last, stop=1, done=mine_done)

    sent_parts = []

    def send_part(time):
        a, b = bounds[len(sent_parts)]
        sent_parts.append(run("part", lambda value: value[a:b], gradient))

    send_part(0)
    Scatter(run, "own", "own", y_first, gradient, gradient, bit, gather("own", "own", y_first, y_last, done=add_own)).start(STARTS["own"])
    for _ in bounds[1:]:
        send_part(0)
    crossed_parts = [[from_row(part, partner(m)) for part in sent_parts] for m in mates]

    below = lambda *values: jnp.concatenate(values, 0)

    def start_beside(time):
        for m, values in zip(mates, crossed_parts):
            crossed[m] = run("crossed_whole", below, *values)
            run.at(time + CROSSED_BESIDE_COST, lambda time, m=m, value=swap(crossed[m]): crossed_beside.__setitem__(m, run.hold(value)))

    run.at(CROSSED_BESIDE_AT, start_beside)
    run.at(STARTS["next"], Scatter(run, "next", "next", z_first, gradient, beside, bit, gather("next", "next", z_first, z_last, done=add_next), twist=core).start)
    for m, parts in zip(mates, crossed_parts):
        for index, part in enumerate(parts):
            run.at(STARTS[f"far_{index}"], Scatter(run, f"far_{m}_{index}", f"far_{index}", y_first, gradient, part, bit, part_done(m, index)).start)
    run.drain()

    own = gathers["own"].block
    whole = run("inner_whole", below, *[inner_parts[i] for i in range(len(bounds))])
    inner_beside = swap(whole)
    turned_wholes = [run("turned_whole", lambda *values: jnp.concatenate(values, 1), *[turned_parts[i][m] for i in range(len(bounds))]) for m in mates]
    outer = None
    rms_scale = math.sqrt(gradient.shape[1] * col_count)
    for index, (a, b) in enumerate(bounds):
        arrived = [run.hold(value) for value in inner_crossed[index]]
        arrived_beside = [swap(value) for value in arrived]
        if outer is None:
            outer = run("outer_own", lambda block, right: product(block, right, PLAIN), own, whole)
            outer = run("outer_next", lambda total, *values: total + checkered(*values, core), outer, *near, inner_beside)
        for m, right in zip(mates, arrived):
            outer = run("outer_far", lambda total, block, right: total + product(block, right, PLAIN), outer, far_blocks[m, index], right)
        for last, block, right in zip([False] * (len(mates) - 1) + [index == len(bounds) - 1], turned_wholes, arrived_beside):

            def finish_outer(total, start, block, right):
                total = total + product(block[a:b], right, LEFT_TURNED)
                return (rms_scale * (A_COEF * start.astype(jnp.float32) + total)).astype(jnp.bfloat16) if last else total

            outer = run("outer_turned", finish_outer, outer, gradient, block, right)
    return outer[:kept_rows]


def solution(mesh):
    spec = P("row", "col")
    return jax.shard_map(shards, mesh=mesh, in_specs=(spec,), out_specs=spec, check_vma=False)
```

```python
import heapq
import math

import jax
import jax.numpy as jnp
from jax import lax
from jax.sharding import PartitionSpec as P

A_COEF = 3.4445
B_COEF = -4.775
C_COEF = 2.0315

ROWS_BY_ROWS = (((1,), (1,)), ((), ()))
PLAIN = (((1,), (0,)), ((), ()))
LEFT_TURNED = (((0,), (0,)), ((), ()))

STARTS = {"own": 0.0, "next": 17.0, "far_0": 30.0, "far_1": 58.0}
SCATTERS = {"own": (40.0, 25.0, 18.0), "next": (24.0, 24.0, 17.0), "far_0": (22.0, 18.0, 15.0), "far_1": (20.0, 13.0, 9.0)}
GATHERS = {"own": (14.0, 18.0, 32.0), "next": (8.0, 20.0, 25.0), "far_0": (11.0, 11.0, 13.0), "far_1": (8.0, 14.0, 20.0)}
DELAYS = {"own": 104.0, "next": 106.0}
OVER_COST = 18.0
CROSSED_BESIDE_AT = 60.0
CROSSED_BESIDE_COST = 18.0
MIRROR_COST = 12.0


def cost(table, kind, step):
    return table[kind][min(step, len(table[kind]) - 1)]


def product(left, right, dims):
    return lax.dot_general(left, right, dims, preferred_element_type=jnp.float32)


def from_row(value, source):
    count = lax.axis_size("row")
    return lax.ppermute(value, "row", [(source(i), i) for i in range(count)])


def from_col(value, mask):
    count = lax.axis_size("col")
    return lax.ppermute(value, "col", [(i ^ mask, i) for i in range(count)])


def swap(value):
    return from_row(value, lambda i: i ^ 1)


def partner(mate):
    top = 1 << (mate.bit_length() - 1)
    return lambda i: i ^ mate ^ (1 if i & top else 0)


def inverse(source, count):
    table = {source(i): i for i in range(count)}
    return table.__getitem__


class Sequence:
    def __init__(self):
        self.last = None
        self.agenda = []
        self.added = 0

    def __call__(self, name, step, *values):
        if self.last is not None:
            values = lax.optimization_barrier((values, self.last))[0]
        with jax.named_scope(name):
            result = step(*values)
        self.last = jax.tree.leaves(result)[0]
        return result

    def hold(self, value):
        value, _ = lax.optimization_barrier((value, self.last))
        self.last = value
        return value

    def tie(self, value):
        return lax.optimization_barrier((value, self.last))[0]

    def at(self, time, step):
        heapq.heappush(self.agenda, (time, self.added, step))
        self.added += 1

    def drain(self):
        while self.agenda:
            time, _, step = heapq.heappop(self.agenda)
            step(time)


def take(value, at, count):
    return lax.dynamic_slice_in_dim(value, at * count, count, 0)


def joined(mine, other, at, axis=0):
    count = mine.shape[axis]
    shape = mine.shape[:axis] + (2 * count,) + mine.shape[axis + 1 :]
    both = lax.dynamic_update_slice_in_dim(jnp.zeros(shape, mine.dtype), mine, at * count, axis)
    if other is None:
        return both
    return lax.dynamic_update_slice_in_dim(both, other, (1 - at) * count, axis)


class Scatter:
    def __init__(self, run, name, kind, masks, left, right, bit, done, twist=None):
        self.run, self.name, self.kind, self.masks, self.left, self.right, self.bit, self.done = run, name, kind, masks, left, right, bit, done
        self.twist = twist

    def start(self, time):
        mask, half = self.masks[0], self.left.shape[0] // 2
        at = self.bit(mask)

        def columns(right, place):
            return right if self.twist is None else take(right, place ^ self.twist, half)

        def sent(left, right):
            return product(take(left, 1 - at, half), columns(right, 1 - at), ROWS_BY_ROWS).astype(jnp.bfloat16)

        def kept(left, right):
            return product(take(left, at, half), columns(right, at), ROWS_BY_ROWS)

        self.got = from_col(self.run(self.name + "_sent", sent, self.left, self.right), mask)
        self.kept = self.run(self.name + "_kept", kept, self.left, self.right)
        self.step = 1
        self.run.at(time + cost(SCATTERS, self.kind, 0), self.halve)

    def halve(self, time):
        if self.step == len(self.masks):
            shard = self.run(self.name + "_shard", lambda kept, got: (kept + got.astype(jnp.float32)).astype(jnp.bfloat16), self.kept, self.got)
            return self.done(time, shard)
        mask, count = self.masks[self.step], self.kept.shape[0] // 2
        at = self.bit(mask)

        def one(kept, got):
            total = kept + got.astype(jnp.float32)
            return take(total, 1 - at, count).astype(jnp.bfloat16), take(total, at, count)

        sent, self.kept = self.run(f"{self.name}_halved_{self.step}", one, self.kept, self.got)
        self.got = from_col(sent, mask)
        self.step += 1
        self.run.at(time + cost(SCATTERS, self.kind, self.step - 1), self.halve)


def checkered(block, right, core):
    half = block.shape[0] // 2
    parts = [product(block[:half], take(right, core, half), PLAIN), product(block[half:], take(right, 1 - core, half), PLAIN)]
    return jnp.concatenate(parts, 0)


def checkered_turned(mirror, right, core):
    half = mirror.shape[0] // 2
    parts = [product(mirror[:half], right[:half], LEFT_TURNED), product(mirror[half:], right[half:], LEFT_TURNED)]
    return jnp.concatenate([jnp.where(core == 0, parts[1], parts[0]), jnp.where(core == 0, parts[0], parts[1])], 0)


class Gather:
    def __init__(self, run, name, kind, masks, steps, bit, shard, done=None, stop=0):
        self.run, self.name, self.kind, self.masks, self.steps, self.bit, self.done, self.stop = run, name, kind, masks, list(steps), bit, done, stop
        self.held = shard.reshape((1,) * len(masks) + shard.shape)
        self.taken = 0

    def start(self, time):
        if self.done is not None and len(self.steps) == self.stop:
            self.done(time)
        if self.steps:
            self.got = from_col(self.held, self.steps[0])
            if len(self.steps) > self.stop:
                self.run.at(time + cost(GATHERS, self.kind, self.taken), self.double)

    def double(self, time):
        mask = self.steps.pop(0)
        axis, at = self.masks.index(mask), self.bit(mask)
        self.held = self.run(f"{self.name}_doubled_{len(self.steps)}", lambda held, got: joined(held, got, at, axis), self.held, self.got)
        self.taken += 1
        self.start(time)

    @property
    def block(self):
        return self.held.reshape(-1, self.held.shape[-1])


def shards(gradient):
    kept_rows = gradient.shape[0]
    row_count = lax.axis_size("row")
    col_count = lax.axis_size("col")
    gradient = jnp.pad(gradient, ((0, -kept_rows % col_count), (0, 0)))
    rows = gradient.shape[0]
    half = rows // 2
    col = lax.axis_index("col")
    masks = [1 << b for b in range(col_count.bit_length() - 1)]
    y_first, z_first = masks, masks[1:] + masks[:1]
    y_last = masks[::-1]
    z_last = masks[:1] + masks[:0:-1]
    mates = range(2, row_count, 2)
    run = Sequence()

    def bit(mask):
        return col // mask % 2

    at = bit(masks[0])
    cut = half // 128 * 128
    bounds = [(0, cut), (cut, rows)] if cut else [(0, rows)]
    beside = swap(gradient)
    gathers = {}
    turned = {}
    near, totals, turned_parts, inner_parts, inner_crossed = [], [], {}, {}, {}
    crossed, crossed_beside = {}, {}
    core = lax.axis_index("row") % 2
    missing = [4 + len(mates) * len(bounds)]

    def add_total(name, step, *values):
        if totals:
            totals[0] = run(name, lambda total, *values: total + step(*values), totals[0], *values)
        else:
            totals.append(run(name, step, *values))
        missing[0] -= 1
        finish_parts()

    def finish_parts():
        for index, (a, b) in enumerate(bounds):
            if missing[0] or index in inner_parts or len(turned_parts.get(index, ())) < len(mates):
                continue

            def finish(total, start, *values):
                total = total[a:b]
                for block, right in zip(values[: len(mates)], values[len(mates) :]):
                    total = total + product(block, right, LEFT_TURNED)
                return (B_COEF * start[a:b].astype(jnp.float32) + C_COEF * total).astype(jnp.bfloat16)

            part = run("inner_part", finish, totals[0], gradient, *[turned_parts[index][m] for m in mates], *[crossed_beside[m] for m in mates])
            inner_parts[index] = part
            inner_crossed[index] = [from_row(part, partner(m)) for m in mates]

    def add_rows(name, block, side):
        def step(total, block, right):
            rows_total = take(total, side, half) + product(block.reshape(half, rows), right, PLAIN)
            return lax.dynamic_update_slice_in_dim(total, rows_total, side * half, 0)

        if totals:
            totals[0] = run(name, step, totals[0], block, gradient)
        else:
            totals.append(run(name, lambda block, right: joined(product(block.reshape(half, rows), right, PLAIN), None, side), block, gradient))
        missing[0] -= 1
        finish_parts()

    def add_own(time):
        piece = gathers["own"]
        add_rows("inner_own_mine", piece.held, at)

        def arrived(time):
            piece.got = run.hold(piece.got)
            add_rows("inner_own_other", piece.got, 1 - at)

        run.at(time + cost(GATHERS, "own", 2), arrived)

    def add_next(time):
        near.append(gathers["next"].block)
        mirror = swap(near[0])
        add_total("inner_next", lambda *values: checkered(*values, core), near[0], beside)

        def add(time):
            near.append(mirror)
            add_total("inner_mirror", lambda *values: checkered_turned(*values, core), mirror, beside)

        run.at(time + MIRROR_COST, add)

    def as_block(mine, other):
        return joined(mine.reshape(half, -1), other.reshape(half, -1), at)

    def gather(name, kind, masks, steps, stop=0, done=None):
        def begin(time, shard):
            piece = gathers[name] = Gather(run, name, kind, masks, steps, bit, shard, stop=stop, done=done)

            def start(time):
                piece.held = run.tie(piece.held)
                piece.start(time)

            if kind in DELAYS:
                run.at(max(time, DELAYS[kind]), start)
            else:
                piece.start(time)

        return begin

    far_blocks = {}

    def part_done(m, index):
        name = f"far_{m}_{index}"
        source = inverse(partner(m), row_count)

        def over(value, time, place):
            moved = from_row(value, source)

            def take_in(time):
                turned[m, index, place] = run.hold(moved)
                if (m, index, 0) in turned and (m, index, 1) in turned:
                    turned_parts.setdefault(index, {})[m] = run("turned_part", as_block, turned[m, index, 0], turned[m, index, 1])
                    finish_parts()

            run.at(time + OVER_COST, take_in)

        def arrived(time):
            piece = gathers[name]
            got = run.hold(piece.got)
            over(got, time, 1)
            far_blocks[m, index] = run("far_block", as_block, piece.held, got)
            a, b = bounds[index]
            add_total("inner_far", lambda block, right: product(block, right[a:b], PLAIN), far_blocks[m, index], crossed[m])

        def mine_done(time):
            over(gathers[name].held, time, 0)
            run.at(time + cost(GATHERS, f"far_{index}", 2), arrived)

        return gather(name, f"far_{index}", y_first, y_last, stop=1, done=mine_done)

    sent_parts = []

    def send_part(time):
        a, b = bounds[len(sent_parts)]
        sent_parts.append(run("part", lambda value: value[a:b], gradient))

    send_part(0)
    Scatter(run, "own", "own", y_first, gradient, gradient, bit, gather("own", "own", y_first, y_last, stop=1, done=add_own)).start(STARTS["own"])
    for _ in bounds[1:]:
        send_part(0)
    crossed_parts = [[from_row(part, partner(m)) for part in sent_parts] for m in mates]

    below = lambda *values: jnp.concatenate(values, 0)

    def start_beside(time):
        for m, values in zip(mates, crossed_parts):
            crossed[m] = run("crossed_whole", below, *values)
            run.at(time + CROSSED_BESIDE_COST, lambda time, m=m, value=swap(crossed[m]): crossed_beside.__setitem__(m, run.hold(value)))

    run.at(CROSSED_BESIDE_AT, start_beside)
    run.at(STARTS["next"], Scatter(run, "next", "next", z_first, gradient, beside, bit, gather("next", "next", z_first, z_last, done=add_next), twist=core).start)
    for m, parts in zip(mates, crossed_parts):
        for index, part in enumerate(parts):
            run.at(STARTS[f"far_{index}"], Scatter(run, f"far_{m}_{index}", f"far_{index}", y_first, gradient, part, bit, part_done(m, index)).start)
    run.drain()

    whole = run("inner_whole", below, *[inner_parts[i] for i in range(len(bounds))])
    inner_beside = swap(whole)
    turned_wholes = [run("turned_whole", lambda *values: jnp.concatenate(values, 1), *[turned_parts[i][m] for i in range(len(bounds))]) for m in mates]
    outer = None
    rms_scale = math.sqrt(gradient.shape[1] * col_count)
    for index, (a, b) in enumerate(bounds):
        arrived = [run.hold(value) for value in inner_crossed[index]]
        arrived_beside = [swap(value) for value in arrived]
        if outer is None:
            outer = run("outer_own", lambda mine, other, right: product(as_block(mine, other), right, PLAIN), gathers["own"].held, gathers["own"].got, whole)
            outer = run("outer_next", lambda total, *values: total + checkered(*values, core), outer, near[0], inner_beside)
            outer = run("outer_mirror", lambda total, *values: total + checkered_turned(*values, core), outer, near[1], inner_beside)
        for m, right in zip(mates, arrived):
            outer = run("outer_far", lambda total, block, right: total + product(block, right, PLAIN), outer, far_blocks[m, index], right)
        for last, block, right in zip([False] * (len(mates) - 1) + [index == len(bounds) - 1], turned_wholes, arrived_beside):

            def finish_outer(total, start, block, right):
                total = total + product(block[a:b], right, LEFT_TURNED)
                return (rms_scale * (A_COEF * start.astype(jnp.float32) + total)).astype(jnp.bfloat16) if last else total

            outer = run("outer_turned", finish_outer, outer, gradient, block, right)
    return outer[:kept_rows]


def solution(mesh):
    spec = P("row", "col")
    return jax.shard_map(shards, mesh=mesh, in_specs=(spec,), out_specs=spec, check_vma=False)
```

```python
import heapq
import math

import jax
import jax.numpy as jnp
from jax import lax
from jax.sharding import PartitionSpec as P

A_COEF = 3.4445
B_COEF = -4.775
C_COEF = 2.0315

ROWS_BY_ROWS = (((1,), (1,)), ((), ()))
PLAIN = (((1,), (0,)), ((), ()))
LEFT_TURNED = (((0,), (0,)), ((), ()))

STARTS = {"own": 0.0, "next": 17.0, "far_0": 30.0, "far_1": 58.0}
SCATTERS = {"own": (40.0, 25.0, 18.0), "next": (24.0, 24.0, 17.0), "far_0": (22.0, 18.0, 15.0), "far_1": (20.0, 13.0, 9.0)}
GATHERS = {"own": (14.0, 18.0, 32.0), "next": (8.0, 20.0, 25.0), "far_0": (11.0, 11.0, 13.0), "far_1": (8.0, 14.0, 20.0)}
DELAYS = {"own": 104.0, "next": 106.0}
OVER_COST = 18.0
CROSSED_BESIDE_AT = 60.0
CROSSED_BESIDE_COST = 18.0
MIRROR_COST = 4.0
CUT = 0.5


def cost(table, kind, step):
    return table[kind][min(step, len(table[kind]) - 1)]


def product(left, right, dims):
    return lax.dot_general(left, right, dims, preferred_element_type=jnp.float32)


def from_row(value, source):
    count = lax.axis_size("row")
    return lax.ppermute(value, "row", [(source(i), i) for i in range(count)])


def from_col(value, mask):
    count = lax.axis_size("col")
    return lax.ppermute(value, "col", [(i ^ mask, i) for i in range(count)])


def swap(value):
    return from_row(value, lambda i: i ^ 1)


def partner(mate):
    top = 1 << (mate.bit_length() - 1)
    return lambda i: i ^ mate ^ (1 if i & top else 0)


def inverse(source, count):
    table = {source(i): i for i in range(count)}
    return table.__getitem__


class Sequence:
    def __init__(self):
        self.last = None
        self.agenda = []
        self.added = 0

    def __call__(self, name, step, *values):
        if self.last is not None:
            values = lax.optimization_barrier((values, self.last))[0]
        with jax.named_scope(name):
            result = step(*values)
        self.last = jax.tree.leaves(result)[0]
        return result

    def hold(self, value):
        value, _ = lax.optimization_barrier((value, self.last))
        self.last = value
        return value

    def tie(self, value):
        return lax.optimization_barrier((value, self.last))[0]

    def at(self, time, step):
        heapq.heappush(self.agenda, (time, self.added, step))
        self.added += 1

    def drain(self):
        while self.agenda:
            time, _, step = heapq.heappop(self.agenda)
            step(time)


def take(value, at, count):
    return lax.dynamic_slice_in_dim(value, at * count, count, 0)


def joined(mine, other, at, axis=0):
    count = mine.shape[axis]
    shape = mine.shape[:axis] + (2 * count,) + mine.shape[axis + 1 :]
    both = lax.dynamic_update_slice_in_dim(jnp.zeros(shape, mine.dtype), mine, at * count, axis)
    if other is None:
        return both
    return lax.dynamic_update_slice_in_dim(both, other, (1 - at) * count, axis)


class Scatter:
    def __init__(self, run, name, kind, masks, left, right, bit, done, twist=None):
        self.run, self.name, self.kind, self.masks, self.left, self.right, self.bit, self.done = run, name, kind, masks, left, right, bit, done
        self.twist = twist

    def start(self, time):
        mask, half = self.masks[0], self.left.shape[0] // 2
        at = self.bit(mask)

        def columns(right, place):
            return right if self.twist is None else take(right, place ^ self.twist, half)

        def sent(left, right):
            return product(take(left, 1 - at, half), columns(right, 1 - at), ROWS_BY_ROWS).astype(jnp.bfloat16)

        def kept(left, right):
            return product(take(left, at, half), columns(right, at), ROWS_BY_ROWS)

        self.got = from_col(self.run(self.name + "_sent", sent, self.left, self.right), mask)
        self.kept = self.run(self.name + "_kept", kept, self.left, self.right)
        self.step = 1
        self.run.at(time + cost(SCATTERS, self.kind, 0), self.halve)

    def halve(self, time):
        if self.step == len(self.masks):
            shard = self.run(self.name + "_shard", lambda kept, got: (kept + got.astype(jnp.float32)).astype(jnp.bfloat16), self.kept, self.got)
            return self.done(time, shard)
        mask, count = self.masks[self.step], self.kept.shape[0] // 2
        at = self.bit(mask)

        def one(kept, got):
            total = kept + got.astype(jnp.float32)
            return take(total, 1 - at, count).astype(jnp.bfloat16), take(total, at, count)

        sent, self.kept = self.run(f"{self.name}_halved_{self.step}", one, self.kept, self.got)
        self.got = from_col(sent, mask)
        self.step += 1
        self.run.at(time + cost(SCATTERS, self.kind, self.step - 1), self.halve)


def checkered(block, right, core):
    half = block.shape[0] // 2
    parts = [product(block[:half], take(right, core, half), PLAIN), product(block[half:], take(right, 1 - core, half), PLAIN)]
    return jnp.concatenate(parts, 0)


def checkered_turned(mirror, right, core):
    half = mirror.shape[0] // 2
    parts = [product(mirror[:half], right[:half], LEFT_TURNED), product(mirror[half:], right[half:], LEFT_TURNED)]
    return jnp.concatenate([jnp.where(core == 0, parts[1], parts[0]), jnp.where(core == 0, parts[0], parts[1])], 0)


class Gather:
    def __init__(self, run, name, kind, masks, steps, bit, shard, done=None, stop=0):
        self.run, self.name, self.kind, self.masks, self.steps, self.bit, self.done, self.stop = run, name, kind, masks, list(steps), bit, done, stop
        self.held = shard.reshape((1,) * len(masks) + shard.shape)
        self.taken = 0

    def start(self, time):
        if self.done is not None and len(self.steps) == self.stop:
            self.done(time)
        if self.steps:
            self.got = from_col(self.held, self.steps[0])
            if len(self.steps) > self.stop:
                self.run.at(time + cost(GATHERS, self.kind, self.taken), self.double)

    def double(self, time):
        mask = self.steps.pop(0)
        axis, at = self.masks.index(mask), self.bit(mask)
        self.held = self.run(f"{self.name}_doubled_{len(self.steps)}", lambda held, got: joined(held, got, at, axis), self.held, self.got)
        self.taken += 1
        self.start(time)

    @property
    def block(self):
        return self.held.reshape(-1, self.held.shape[-1])


def shards(gradient):
    kept_rows = gradient.shape[0]
    row_count = lax.axis_size("row")
    col_count = lax.axis_size("col")
    gradient = jnp.pad(gradient, ((0, -kept_rows % col_count), (0, 0)))
    rows = gradient.shape[0]
    half = rows // 2
    col = lax.axis_index("col")
    masks = [1 << b for b in range(col_count.bit_length() - 1)]
    y_first, z_first = masks, masks[1:] + masks[:1]
    y_last = masks[::-1]
    z_last = masks[:1] + masks[:0:-1]
    mates = range(2, row_count, 2)
    run = Sequence()

    def bit(mask):
        return col // mask % 2

    at = bit(masks[0])
    cut = int(rows * CUT) // 128 * 128
    bounds = [(0, cut), (cut, rows)] if cut else [(0, rows)]
    beside = swap(gradient)
    gathers = {}
    turned = {}
    near, near_totals, totals, turned_parts, inner_parts, inner_crossed = [], [], [], {}, {}, {}
    crossed, crossed_beside = {}, {}
    core = lax.axis_index("row") % 2
    missing = [3 + len(mates) * len(bounds)]

    def add_total(name, step, *values):
        if totals:
            totals[0] = run(name, lambda total, *values: total + step(*values), totals[0], *values)
        else:
            totals.append(run(name, step, *values))
        missing[0] -= 1
        finish_parts()

    def finish_parts():
        for index, (a, b) in enumerate(bounds):
            if missing[0] or index in inner_parts or len(turned_parts.get(index, ())) < len(mates):
                continue

            def finish(total, near_total, start, *values):
                total = total[a:b] + near_total[a:b]
                for block, right in zip(values[: len(mates)], values[len(mates) :]):
                    total = total + product(block, right, LEFT_TURNED)
                return (B_COEF * start[a:b].astype(jnp.float32) + C_COEF * total).astype(jnp.bfloat16)

            part = run("inner_part", finish, totals[0], near_totals[0], gradient, *[turned_parts[index][m] for m in mates], *[crossed_beside[m] for m in mates])
            inner_parts[index] = part
            inner_crossed[index] = [from_row(part, partner(m)) for m in mates]

    def add_rows(name, block, side):
        def step(total, block, right):
            rows_total = take(total, side, half) + product(block.reshape(half, rows), right, PLAIN)
            return lax.dynamic_update_slice_in_dim(total, rows_total, side * half, 0)

        if totals:
            totals[0] = run(name, step, totals[0], block, gradient)
        else:
            totals.append(run(name, lambda block, right: joined(product(block.reshape(half, rows), right, PLAIN), None, side), block, gradient))
        missing[0] -= 1
        finish_parts()

    def add_own(time):
        piece = gathers["own"]
        add_rows("inner_own_mine", piece.held, at)

        def arrived(time):
            piece.got = run.hold(piece.got)
            add_rows("inner_own_other", piece.got, 1 - at)

        run.at(time + cost(GATHERS, "own", 2), arrived)

    def add_next(time):
        near.append(gathers["next"].block)
        mirror = swap(near[0])
        near_total = run("inner_next", lambda *values: checkered(*values, core), near[0], beside)

        def add(time):
            near.append(mirror)
            near_totals.append(run("inner_mirror", lambda total, *values: total + checkered_turned(*values, core), near_total, mirror, beside))
            missing[0] -= 1
            finish_parts()

        run.at(time + MIRROR_COST, add)

    def as_block(mine, other):
        return joined(mine.reshape(half, -1), other.reshape(half, -1), at)

    def gather(name, kind, masks, steps, stop=0, done=None):
        def begin(time, shard):
            piece = gathers[name] = Gather(run, name, kind, masks, steps, bit, shard, stop=stop, done=done)

            def start(time):
                piece.held = run.tie(piece.held)
                piece.start(time)

            if kind in DELAYS:
                run.at(max(time, DELAYS[kind]), start)
            else:
                piece.start(time)

        return begin

    far_blocks = {}

    def part_done(m, index):
        name = f"far_{m}_{index}"
        source = inverse(partner(m), row_count)

        def over(value, time, place):
            moved = from_row(value, source)

            def take_in(time):
                turned[m, index, place] = run.hold(moved)
                if (m, index, 0) in turned and (m, index, 1) in turned:
                    turned_parts.setdefault(index, {})[m] = run("turned_part", as_block, turned[m, index, 0], turned[m, index, 1])
                    finish_parts()

            run.at(time + OVER_COST, take_in)

        def arrived(time):
            piece = gathers[name]
            got = run.hold(piece.got)
            over(got, time, 1)
            far_blocks[m, index] = run("far_block", as_block, piece.held, got)
            a, b = bounds[index]
            add_total("inner_far", lambda block, right: product(block, right[a:b], PLAIN), far_blocks[m, index], crossed[m])

        def mine_done(time):
            over(gathers[name].held, time, 0)
            run.at(time + cost(GATHERS, f"far_{index}", 2), arrived)

        return gather(name, f"far_{index}", y_first, y_last, stop=1, done=mine_done)

    sent_parts = []

    def send_part(time):
        a, b = bounds[len(sent_parts)]
        sent_parts.append(run("part", lambda value: value[a:b], gradient))

    send_part(0)
    Scatter(run, "own", "own", y_first, gradient, gradient, bit, gather("own", "own", y_first, y_last, stop=1, done=add_own)).start(STARTS["own"])
    for _ in bounds[1:]:
        send_part(0)
    crossed_parts = [[from_row(part, partner(m)) for part in sent_parts] for m in mates]

    below = lambda *values: jnp.concatenate(values, 0)

    def start_beside(time):
        for m, values in zip(mates, crossed_parts):
            crossed[m] = run("crossed_whole", below, *values)
            run.at(time + CROSSED_BESIDE_COST, lambda time, m=m, value=swap(crossed[m]): crossed_beside.__setitem__(m, run.hold(value)))

    run.at(CROSSED_BESIDE_AT, start_beside)
    run.at(STARTS["next"], Scatter(run, "next", "next", z_first, gradient, beside, bit, gather("next", "next", z_first, z_last, done=add_next), twist=core).start)
    for m, parts in zip(mates, crossed_parts):
        for index, part in enumerate(parts):
            run.at(STARTS[f"far_{index}"], Scatter(run, f"far_{m}_{index}", f"far_{index}", y_first, gradient, part, bit, part_done(m, index)).start)
    run.drain()

    whole = run("inner_whole", below, *[inner_parts[i] for i in range(len(bounds))])
    inner_beside = swap(whole)
    turned_wholes = [run("turned_whole", lambda *values: jnp.concatenate(values, 1), *[turned_parts[i][m] for i in range(len(bounds))]) for m in mates]
    outer = None
    rms_scale = math.sqrt(gradient.shape[1] * col_count)
    for index, (a, b) in enumerate(bounds):
        arrived = [run.hold(value) for value in inner_crossed[index]]
        arrived_beside = [swap(value) for value in arrived]
        if outer is None:
            outer = run("outer_own", lambda start, mine, other, right: A_COEF * start.astype(jnp.float32) + product(as_block(mine, other), right, PLAIN), gradient, gathers["own"].held, gathers["own"].got, whole)
            outer = run("outer_next", lambda total, *values: total + checkered(*values, core), outer, near[0], inner_beside)
            outer = run("outer_mirror", lambda total, *values: total + checkered_turned(*values, core), outer, near[1], inner_beside)
        for m, right in zip(mates, arrived):
            outer = run("outer_far", lambda total, block, right: total + product(block, right, PLAIN), outer, far_blocks[m, index], right)
        for last, block, right in zip([False] * (len(mates) - 1) + [index == len(bounds) - 1], turned_wholes, arrived_beside):

            def finish_outer(total, block, right):
                total = total + product(block[a:b], right, LEFT_TURNED)
                return (rms_scale * total).astype(jnp.bfloat16) if last else total

            outer = run("outer_turned", finish_outer, outer, block, right)
    return outer[:kept_rows]


def solution(mesh):
    spec = P("row", "col")
    return jax.shard_map(shards, mesh=mesh, in_specs=(spec,), out_specs=spec, check_vma=False)
```
